32 devices in a mesh: groups: 2 (over x), tok: 16 (over z, y, core).
Axes of the slice: x: 2, y: 2, z: 4, core: 2. Of those that a mesh axis runs over, the one named last changes fastest.
Arguments:
- vis_query: bfloat16 [8192, 1280], P(('groups', 'tok')), parts along dimension 0, may hold values from -180 to 180
- vis_keyvalue: bfloat16 [2, 8192, 1280], P(None, ('groups', 'tok')), parts along dimension 1, may hold values from -6 to 6
- vis_residual: bfloat16 [8192, 1280], P(('groups', 'tok')), parts along dimension 0, may hold values from -4 to 4
- vis_out_weight: bfloat16 [1280, 1280], P('tok'), may hold values from -0.15625 to 0.15625
- vis_out_bias: float32 [1280], replicated, may hold values from -4 to 4
- image_units: int32 [96], P('groups'), parts along dimension 0, may hold values from 1 to 32, 1024 in all
- text_embed: bfloat16 [8192, 5120], P(('groups', 'tok')), parts along dimension 0, may hold values from -6 to 6
- lm_gain: float32 [5120], replicated, may hold values from 0.1 to 1.9
- lm_kv_weight: bfloat16 [5120, 2048], P(None, 'tok'), may hold values from -0.078125 to 0.078125
- lm_kv_bias: float32 [2048], replicated, may hold values from -6 to 6
- text_positions: int32 [8192], P(('groups', 'tok')), parts along dimension 0, may hold values from 0 to 4095
- image_destination: int32 [2048, 1], P(('groups', 'tok')), parts along dimension 0, may hold values from 0 to 15; in each aligned block of 64 rows (0 to 63, 64 to 127, ...) at most 8 rows name the same one
- image_positions: int32 [3, 4096], P(None, ('groups', 'tok')), parts along dimension 1, may hold values from 0 to 4095
Outputs:
- text_cache: bfloat16 [8192, 2048], P(('groups', 'tok')), parts along dimension 0
- image_cache: bfloat16 [4096, 2048], P(('groups', 'tok')), parts along dimension 0
The draws below stay inside these ranges and needn't reach their ends.
There are 2 independent parts, one for each index of `groups`. The reference program is written for one: setup_inputs(seed, part) draws one part's arguments, and reference() takes and returns one part's arrays. A program takes and returns all parts, laid end to end along the dimension named above; an argument that names none is the same for every part. Nothing has to cross between parts.
Inputs may be any that keep to these rules, and one draw needn't show every extreme that they name: `image_units`: each image spans whole merged rows; entries sum to 1024 and one reaches the largest value. `image_destination`: among the 64 rows of one device no destination appears more than 8 times, and some device's rows reach that count.
All inputs are finite; a program needn't handle non-finite values.
Results may differ from the reference program's by a relative error of at most 0.0052.
Values may be sent and summed in bfloat16 or wider, within the bound.
A program may use at most 128 MiB of HBM per device.

```python
import math
import jax
import jax.numpy as jnp
import numpy as np
from jax import lax

VIS_WIDTH = 1280
VIS_HEADS = 16
KV_HEADS = 8
LM_HEAD = 128
LM_WIDTH = 5120
KV_WIDTH = 2048
PATCH_DEV = 256
POS_LIMIT = 4096
UNITS_DEV = 64
CAP = 8
SLOTS_DEV = 128
PATCHES = 4096
UNITS = 1024
TEXT = 4096
IMG_SLOTS = 2048
IMAGES = 48
DESTS = 16
N_TOK = 16


def draw_keys(key):
    keys = jnp.clip(jax.random.normal(jax.random.fold_in(key, 7001), (PATCHES, VIS_WIDTH), jnp.float32), -6.0, 6.0)
    return keys


def draw_vis_keyvalue(key, part):
    keys = draw_keys(key)
    values = jnp.clip(jax.random.normal(jax.random.fold_in(key, 7004), (PATCHES, VIS_WIDTH), jnp.float32), -6.0, 6.0)
    return jnp.stack([keys, values]).astype(jnp.bfloat16)


def draw_vis_query(key, part):
    fresh = jnp.clip(jax.random.normal(jax.random.fold_in(key, 7002), (PATCHES, VIS_WIDTH), jnp.float32), -6.0, 6.0)
    return fresh.astype(jnp.bfloat16)


def set_ends(values, rng, least, largest):
    place = [jax.random.randint(jax.random.fold_in(rng, axis), (), 0, length) for axis, length in enumerate(values.shape)]
    widest = values.shape.index(max(values.shape))
    neighbour = place[:widest] + [(place[widest] + 1) % values.shape[widest]] + place[widest + 1:]
    return values.at[tuple(place)].set(least).at[tuple(neighbour)].set(largest)


def block_scale(stream_key, shape, shards, low, high):
    level, own = 1.0, jax.random.fold_in(stream_key, 6)
    for dim, shards_of in shards:
        draws = jnp.exp(jax.random.uniform(jax.random.fold_in(own, dim), (shards_of,), jnp.float32, low / len(shards), high / len(shards)))
        level = level * jnp.repeat(draws, shape[dim] // shards_of).reshape([-1 if axis == dim else 1 for axis in range(len(shape))])
    return level


def profile(count, total, reach, lean):
    weights = [(1 << 20) // math.isqrt(standing ** lean) + 1 for standing in range(2, count + 1)]
    surplus, counts = total - reach - (count - 1), [1] * (count - 1)
    while surplus > 0:
        candidates = [i for i in range(count - 1) if counts[i] < reach]
        whole, left = sum([weights[i] for i in candidates]), surplus
        for i in candidates:
            more = min(reach - counts[i], max(1, left * weights[i] // whole), surplus)
            counts[i] = counts[i] + more
            surplus = surplus - more
    return np.array([reach] + counts)


def uneven_parts(key, count, total, reach, lean):
    if count == 2:
        one = jax.random.randint(key, (), max(1, total - reach), min(reach, total - 1) + 1)
        return jnp.stack([one, total - one])
    tallies = jnp.asarray(profile(count, total, reach, lean), jnp.int32)
    pairs = (count - 1) // 2
    giver, sink = tallies[1:1 + 2 * pairs:2], tallies[2:2 + 2 * pairs:2]
    room = jnp.minimum(giver - 1, reach - sink)
    moved = jax.random.randint(jax.random.fold_in(key, 1), (pairs,), 0, 1 << 20) % (room + 1)
    tallies = tallies.at[1:1 + 2 * pairs:2].set(giver - moved).at[2:2 + 2 * pairs:2].set(sink + moved)
    return tallies[jax.random.permutation(jax.random.fold_in(key, 2), count)]


def deal_out(rng, own, number, rows, number_of, top, most, slope):
    order = jax.random.permutation(rng, number_of)
    heavy_load, usual = shares(number_of, rows * top, most, slope, True), shares(number_of, rows * top, most, slope, False)
    places = jnp.arange(number_of)

    def named(tallies, rotation):
        used = int((tallies > 0).sum())
        fixed = max(1, used // 4)
        moved = fixed + (places - fixed + rotation * (used - fixed)) % max(1, number_of - fixed)
        return jnp.zeros((number_of,), jnp.int32).at[order[jnp.where(places < fixed, places, moved)]].set(jnp.asarray(tallies, jnp.int32))

    tallies = jnp.where(number % 4 == 0, named(heavy_load, number // 4), named(usual, number - number // 4 - 1))
    mixed = jax.random.permutation(jax.random.fold_in(own, 3), number_of)
    donor, receiver = mixed[0:number_of // 2 * 2:2], mixed[1:number_of // 2 * 2:2]
    room = jnp.minimum(tallies[donor] - 1, most - tallies[receiver]) // 2
    room = jnp.where((donor == order[0]) | (receiver == order[0]) | (tallies[receiver] == 0), 0, jnp.maximum(room, 0))
    moved = jax.random.randint(jax.random.fold_in(own, 4), (number_of // 2,), 0, 1 << 20) % (room + 1)
    tallies = tallies.at[donor].add(-moved).at[receiver].add(moved)
    items = jnp.searchsorted(jnp.cumsum(tallies), jnp.arange(rows * top), side="right").astype(jnp.int32)
    grid = items.reshape(top, rows).T
    grid = grid[jax.random.permutation(jax.random.fold_in(own, 1), rows)]
    rotation = jax.random.randint(jax.random.fold_in(own, 2), (rows, 1), 0, top)
    return jnp.take_along_axis(grid, (jnp.arange(top)[None, :] + rotation) % top, axis=1)


def shares(count, total, bound, lean, full):
    portions = [(1 << 20) // math.isqrt(standing ** lean) + 1 for standing in range(1, count + 1)]
    largest = bound if full else min(bound, max(-(-total // count), total * portions[0] // sum(portions)))
    least = 1 if total - largest >= count - 1 else 0
    counts, rest = [largest] + [least] * (count - 1), total - largest - least * (count - 1)
    while rest > 0:
        candidates = [i for i in range(1, count) if counts[i] < largest] or [i for i in range(1, count) if counts[i] < bound]
        whole, budget = sum([portions[i] for i in candidates]), rest
        for i in candidates:
            extra = min(bound - counts[i], max(1, budget * portions[i] // whole), rest)
            counts[i] = counts[i] + extra
            rest = rest - extra
    return np.array(counts)


def centred(own_key, dims, deviation, limit, pieces=(), held_as=jnp.bfloat16):
    loudness = block_scale(own_key, dims, pieces, -0.22, 0.18) if pieces else 1.0
    array = jax.random.normal(own_key, dims, jnp.float32) * deviation * loudness
    return jnp.minimum(jnp.maximum(array, -limit), limit).astype(held_as)


def setup_inputs(seed: int = 0, part: int = 0) -> dict:
    seeds = jax.random.split(jax.random.key(seed), 14)
    part_splits = jax.random.split(jax.random.fold_in(seeds[13], part), 14)
    vis_query = draw_vis_query(jax.random.fold_in(jax.random.fold_in(seeds[13], part), 71), part)
    vis_keyvalue = draw_vis_keyvalue(jax.random.fold_in(jax.random.fold_in(seeds[13], part), 71), part)
    vis_residual = centred(part_splits[2], (PATCHES, VIS_WIDTH), 0.3, 4.0, ((0, 16),))
    vis_out_weight = centred(seeds[3], (VIS_WIDTH, VIS_WIDTH), VIS_WIDTH ** -0.5, 0.15625, ((0, 16),))
    vis_out_bias = centred(seeds[4], (VIS_WIDTH,), 0.3, 4.0, (), jnp.float32)
    image_units = uneven_parts(part_splits[5], IMAGES, UNITS, UNITS_DEV // 2, 2).astype(jnp.int32)
    text_embed = centred(part_splits[6], (TEXT, LM_WIDTH), 1.0, 6.0, ((0, 16),))
    lm_gain = jnp.clip(1.0 + 0.18 * jax.random.normal(seeds[7], (LM_WIDTH,), jnp.float32), 0.1, 1.9)
    lm_kv_weight = centred(seeds[8], (LM_WIDTH, KV_WIDTH), LM_WIDTH ** -0.5, 0.078125, ((1, 16),))
    lm_kv_bias = centred(seeds[9], (KV_WIDTH,), 0.5, 6.0, (), jnp.float32)
    text_positions = set_ends(jax.random.randint(part_splits[10], (TEXT,), 0, POS_LIMIT), jax.random.fold_in(part_splits[10], 1), 0, POS_LIMIT - 1).astype(jnp.int32)
    image_destination_keys = jax.random.split(jax.random.fold_in(part_splits[11], 1), UNITS // UNITS_DEV)
    image_destination_turns = jax.random.permutation(jax.random.fold_in(part_splits[11], 3), UNITS // UNITS_DEV)
    image_destination = jax.vmap(lambda own, number: deal_out(jax.random.fold_in(part_splits[11], 2), own, number, UNITS_DEV, DESTS, 1, CAP, 2))(image_destination_keys, image_destination_turns).reshape((UNITS, 1))
    image_positions = set_ends(jax.random.randint(part_splits[12], (3, IMG_SLOTS), 0, POS_LIMIT), jax.random.fold_in(part_splits[12], 1), 0, POS_LIMIT - 1).astype(jnp.int32)
    return dict(vis_query=vis_query, vis_keyvalue=vis_keyvalue, vis_residual=vis_residual, vis_out_weight=vis_out_weight, vis_out_bias=vis_out_bias, image_units=image_units, text_embed=text_embed, lm_gain=lm_gain, lm_kv_weight=lm_kv_weight, lm_kv_bias=lm_kv_bias, text_positions=text_positions, image_destination=image_destination, image_positions=image_positions)


norm_epsilon = 1e-06
rope_base = 1000000.0

def segment_ids(global_index, bounds):
    return lax.optimization_barrier(jnp.sum((global_index[:, None] >= bounds[None, :]).astype(jnp.int32), axis=1)) - 1

def rms_scale(rows, gain):
    values = rows.astype(jnp.float32)
    mean_square = lax.optimization_barrier(jnp.mean(values * values, axis=1, keepdims=True))
    return (values * lax.rsqrt(mean_square + norm_epsilon) * gain).astype(jnp.bfloat16)

def rotate_keys(values, bias, positions):
    shifted = values + bias
    row_count = shifted.shape[0]
    kv_half = shifted.shape[1] // 2
    half_size = LM_HEAD // 2
    key_part = shifted[:, :kv_half].reshape(row_count, KV_HEADS, LM_HEAD)
    lower_half = key_part[:, :, :half_size]
    upper_half = key_part[:, :, half_size:]
    index_pair = jnp.arange(half_size, dtype=jnp.int32)
    frequency = jnp.power(jnp.float32(rope_base), -2.0 * index_pair.astype(jnp.float32) / LM_HEAD)
    section = (index_pair >= half_size // 4).astype(jnp.int32) + (index_pair >= half_size // 4 + 3 * half_size // 8).astype(jnp.int32)
    places = positions.astype(jnp.float32)
    chosen = jnp.zeros((row_count, half_size), jnp.float32)
    for axis_number in range(3):
        chosen = chosen + places[axis_number][:, None] * (section == axis_number).astype(jnp.float32)[None, :]
    angles = chosen * frequency[None, :]
    cosine = jnp.cos(angles)[:, None, :]
    sine_part = jnp.sin(angles)[:, None, :]
    turned = jnp.concatenate([lower_half * cosine - upper_half * sine_part, upper_half * cosine + lower_half * sine_part], axis=2)
    return jnp.concatenate([turned.reshape(row_count, kv_half), shifted[:, kv_half:]], axis=1).astype(jnp.bfloat16)

def reference(vis_query, vis_keyvalue, vis_residual, vis_out_weight, vis_out_bias, image_units, text_embed, lm_gain, lm_kv_weight, lm_kv_bias, text_positions, image_destination, image_positions):
    head_size = VIS_WIDTH // VIS_HEADS
    half_window = PATCH_DEV // 2
    bounds = jnp.concatenate([jnp.zeros((1,), jnp.int32), jnp.cumsum(4 * image_units).astype(jnp.int32)])
    margin = jnp.zeros((2, half_window, VIS_WIDTH), jnp.bfloat16)
    padded = jnp.concatenate([margin, vis_keyvalue, margin], axis=1)
    score_scale = 1.0 / math.sqrt(head_size)

    def one_block(block):
        offset = (block * PATCH_DEV).astype(jnp.int32)
        queries = lax.dynamic_slice_in_dim(vis_query, offset, PATCH_DEV, 0).astype(jnp.float32).reshape(PATCH_DEV, VIS_HEADS, head_size)
        nearby = lax.dynamic_slice_in_dim(padded, offset, 2 * PATCH_DEV, 1).astype(jnp.float32).reshape(2, 2 * PATCH_DEV, VIS_HEADS, head_size)
        query_ids = segment_ids(offset + jnp.arange(PATCH_DEV, dtype=jnp.int32), bounds)
        key_ids = segment_ids(offset - half_window + jnp.arange(2 * PATCH_DEV, dtype=jnp.int32), bounds)
        allowed = query_ids[:, None] == key_ids[None, :]
        scores = jnp.einsum('qhd,khd->hqk', queries, nearby[0]) * score_scale
        scores = jnp.where(allowed[None], scores, -1e+30)
        row_max = lax.optimization_barrier(jnp.max(scores, axis=2, keepdims=True))
        shifted = jnp.exp(scores - row_max)
        weights = (shifted / lax.optimization_barrier(jnp.sum(shifted, axis=2, keepdims=True))).astype(jnp.bfloat16)
        weights = lax.optimization_barrier(weights).astype(jnp.float32)
        mixed = jnp.einsum('hqk,khd->qhd', weights, nearby[1])
        return mixed.astype(jnp.bfloat16).reshape(PATCH_DEV, VIS_WIDTH)
    attended = lax.map(one_block, jnp.arange(N_TOK, dtype=jnp.int32)).reshape(PATCHES, VIS_WIDTH)
    projected = jnp.dot(attended, vis_out_weight, preferred_element_type=jnp.float32)
    vis_hidden = (projected + vis_out_bias + vis_residual.astype(jnp.float32)).astype(jnp.bfloat16)
    merged = vis_hidden.reshape(UNITS, LM_WIDTH)
    image_rows = jnp.dot(rms_scale(merged, lm_gain), lm_kv_weight, preferred_element_type=jnp.float32)
    target = image_destination[:, 0].reshape(N_TOK, UNITS_DEV)
    same_target = target[:, :, None] == target[:, None, :]
    earlier = jnp.arange(UNITS_DEV, dtype=jnp.int32)[None, :] < jnp.arange(UNITS_DEV, dtype=jnp.int32)[:, None]
    slot_rank = lax.optimization_barrier(jnp.sum((same_target & earlier[None]).astype(jnp.int32), axis=2))
    source = jnp.arange(N_TOK, dtype=jnp.int32)[:, None]
    slot_index = (target * SLOTS_DEV + source * CAP + slot_rank).reshape(UNITS).astype(jnp.int32)
    image_values = jnp.zeros((IMG_SLOTS, KV_WIDTH), jnp.float32).at[slot_index].set(image_rows)
    image_cache = rotate_keys(image_values, lm_kv_bias, image_positions)
    text_values = jnp.dot(rms_scale(text_embed, lm_gain), lm_kv_weight, preferred_element_type=jnp.float32)
    text_cache = rotate_keys(text_values, lm_kv_bias, jnp.broadcast_to(text_positions[None, :], (3, TEXT)))
    return (text_cache, image_cache)
```

```python
import functools
import math

import jax
import jax.numpy as jnp
from jax import lax
from jax.experimental import pallas as pl
from jax.experimental.pallas import tpu as pltpu
from jax.sharding import PartitionSpec as P

VIS_HEADS = 16
KV_HEADS = 8
LM_HEAD = 128


norm_epsilon = 1e-06
rope_base = 1000000.0


def with_halo(block, sides, width):
    for axis, dim in sides:
        count = lax.axis_size(axis)
        forward = [(i, i + 1) for i in range(count - 1)]
        backward = [(target, source) for source, target in forward]
        low = lax.ppermute(
            lax.slice_in_dim(block, block.shape[dim] - width, None, axis=dim), axis, forward
        )
        high = lax.ppermute(lax.slice_in_dim(block, 0, width, axis=dim), axis, backward)
        block = jnp.concatenate([low, block, high], axis=dim)
    return block


def running_sums(counts):
    index = jnp.arange(counts.shape[0], dtype=jnp.int32)
    return jnp.sum(jnp.where(index[None, :] <= index[:, None], counts[None, :], 0), axis=1)


def segment_ids(global_index, bounds):
    return jnp.sum((global_index[:, None] >= bounds[None, :]).astype(jnp.int32), axis=1) - 1


def rms_scale(rows, gain):
    values = rows.astype(jnp.float32)
    mean_square = jnp.mean(values * values, axis=1, keepdims=True)
    return (values * lax.rsqrt(mean_square + norm_epsilon) * gain).astype(jnp.bfloat16)


def rotate_keys(values, bias, positions):
    shifted = values + bias
    row_count = shifted.shape[0]
    kv_half = shifted.shape[1] // 2
    half_size = LM_HEAD // 2
    key_part = shifted[:, :kv_half].reshape(row_count, KV_HEADS, LM_HEAD)
    lower_half = key_part[:, :, :half_size]
    upper_half = key_part[:, :, half_size:]
    index_pair = jnp.arange(half_size, dtype=jnp.int32)
    frequency = jnp.power(jnp.float32(rope_base), -2.0 * index_pair.astype(jnp.float32) / LM_HEAD)
    section = (index_pair >= half_size // 4).astype(jnp.int32) + (
        index_pair >= half_size // 4 + 3 * half_size // 8
    ).astype(jnp.int32)
    places = positions.astype(jnp.float32)
    chosen = jnp.zeros((row_count, half_size), jnp.float32)
    for axis_number in range(3):
        chosen = (
            chosen
            + places[axis_number][:, None] * (section == axis_number).astype(jnp.float32)[None, :]
        )
    angles = chosen * frequency[None, :]
    cosine = jnp.cos(angles)[:, None, :]
    sine_part = jnp.sin(angles)[:, None, :]
    turned = jnp.concatenate(
        [
            lower_half * cosine - upper_half * sine_part,
            upper_half * cosine + lower_half * sine_part,
        ],
        axis=2,
    )
    return jnp.concatenate(
        [turned.reshape(row_count, kv_half), shifted[:, kv_half:]], axis=1
    ).astype(jnp.bfloat16)


def head_attention(query_head, key_head, value_head, allowed, score_scale):
    scores = (
        jnp.einsum("qd,kd->qk", query_head, key_head, preferred_element_type=jnp.float32)
        * score_scale
    )
    scores = jnp.where(allowed, scores, -1e30)
    row_max = jnp.max(scores, axis=1, keepdims=True)
    shifted = jnp.exp(scores - row_max)
    weights = (shifted / jnp.sum(shifted, axis=1, keepdims=True)).astype(jnp.bfloat16)
    return jnp.dot(weights, value_head, preferred_element_type=jnp.float32).astype(jnp.bfloat16)


def project_rows(normed, kv_weight):
    return jnp.dot(
        normed,
        lax.all_gather(kv_weight, "tok", axis=1, tiled=True),
        preferred_element_type=jnp.float32,
    )


def per_device(
    vis_query,
    vis_keyvalue,
    vis_residual,
    vis_out_weight,
    vis_out_bias,
    image_units,
    text_embed,
    lm_gain,
    lm_kv_weight,
    lm_kv_bias,
    text_positions,
    image_destination,
    image_positions,
):
    patch_count, vis_width = vis_query.shape
    head_size = vis_width // VIS_HEADS
    half_window = patch_count // 2
    device_count = lax.axis_size("tok")
    device_index = lax.axis_index("tok")
    nearby = with_halo(vis_keyvalue, (("tok", 1),), half_window)
    bounds = jnp.concatenate([jnp.zeros((1,), jnp.int32), running_sums(4 * image_units)])
    offset = device_index * patch_count
    query_ids = segment_ids(offset + jnp.arange(patch_count, dtype=jnp.int32), bounds)
    key_ids = segment_ids(
        offset - half_window + jnp.arange(2 * patch_count, dtype=jnp.int32), bounds
    )
    allowed = query_ids[:, None] == key_ids[None, :]
    score_scale = 1.0 / math.sqrt(head_size)
    query_heads = vis_query.reshape(patch_count, VIS_HEADS, head_size).transpose(1, 0, 2)
    key_heads = nearby[0].reshape(2 * patch_count, VIS_HEADS, head_size).transpose(1, 0, 2)
    value_heads = nearby[1].reshape(2 * patch_count, VIS_HEADS, head_size).transpose(1, 0, 2)
    attended = lax.map(
        lambda pieces: head_attention(pieces[0], pieces[1], pieces[2], allowed, score_scale),
        (query_heads, key_heads, value_heads),
    )
    attended = attended.transpose(1, 0, 2).reshape(patch_count, vis_width)
    projected = jnp.dot(
        attended,
        lax.all_gather(vis_out_weight, "tok", axis=0, tiled=True),
        preferred_element_type=jnp.float32,
    )
    vis_hidden = (projected + vis_out_bias + vis_residual.astype(jnp.float32)).astype(jnp.bfloat16)
    merged = vis_hidden.reshape(patch_count // 4, 4 * vis_width)
    target = image_destination[:, 0]
    unit_count = target.shape[0]
    same_target = target[:, None] == target[None, :]
    earlier = (
        jnp.arange(unit_count, dtype=jnp.int32)[None, :]
        < jnp.arange(unit_count, dtype=jnp.int32)[:, None]
    )
    slot_rank = jnp.sum((same_target & earlier).astype(jnp.int32), axis=1)
    slot_count = image_positions.shape[1]
    capacity = slot_count // device_count
    slot_index = target * capacity + slot_rank
    text_count = text_embed.shape[0]
    kv_width = lm_kv_bias.shape[0]
    normed = rms_scale(jnp.concatenate([text_embed, merged], axis=0), lm_gain)
    projected_rows = project_rows(normed, lm_kv_weight)
    text_values = projected_rows[:text_count]
    outgoing = (
        jnp.zeros((slot_count, kv_width), jnp.float32)
        .at[slot_index]
        .set(projected_rows[text_count:])
    )
    image_values = lax.all_to_all(outgoing, "tok", split_axis=0, concat_axis=0, tiled=True)
    text_cache = rotate_keys(
        text_values, lm_kv_bias, jnp.broadcast_to(text_positions[None, :], (3, text_count))
    )
    image_cache = rotate_keys(image_values, lm_kv_bias, image_positions)
    return (text_cache, image_cache)


MESH = pl.DeviceIdType.MESH


def fused_kernel(
    dims,
    query_ref,
    keyvalue_ref,
    residual_ref,
    out_bias_ref,
    query_id_ref,
    key_id_ref,
    place_ref,
    gain_ref,
    bias_ref,
    cosine_ref,
    sine_ref,
    text_ref,
    out_shard_ref,
    kv_shard_ref,
    text_cache_ref,
    image_cache_ref,
    out_weight,
    kv_weight,
    nearby,
    attended,
    text_rows,
    rows,
    outgoing,
    incoming,
    total,
    sib_send,
    x_send,
    y_send,
    z_send,
    recv,
    halo_send,
    halo_recv,
    row_send,
    row_recv,
    local,
):
    count, depth = dims
    group = lax.axis_index("groups")
    me = lax.axis_index("tok")
    core = lax.rem(me, 2)
    chip = me // 2
    y = lax.rem(chip, 2)
    z = chip // 2
    x = group
    sibling = (group, me + 1 - 2 * core)
    x_peer = (1 - group, me)
    y_peer = (group, me + 2 - 4 * y)
    right = lax.rem(me + 1, count)
    left = lax.rem(me + count - 1, count)
    patches, vis_width = query_ref.shape
    window = patches // 2
    text_count, width = text_ref.shape
    slots = image_cache_ref.shape[0]

    def along(step):
        return lax.rem(z + step, depth)

    def shard_of(level, row, lane):
        return (level * 2 + row) * 2 + lane

    copies = [
        pltpu.make_async_copy(out_shard_ref, out_weight.at[me], local.at[0]),
        pltpu.make_async_copy(kv_shard_ref, kv_weight.at[me], local.at[1]),
        pltpu.make_async_copy(
            keyvalue_ref, nearby.at[:, pl.ds(window, patches), :], local.at[2]
        ),
        pltpu.make_async_copy(text_ref, text_rows, local.at[3]),
    ]
    for copy in copies:
        copy.start()

    barrier = pltpu.get_barrier_semaphore()
    for step in range(1, count):
        pl.semaphore_signal(
            barrier,
            inc=1,
            device_id=(group, lax.rem(me + step, count)),
            device_id_type=MESH,
        )
    pl.semaphore_signal(barrier, inc=1, device_id=x_peer, device_id_type=MESH)
    pl.semaphore_wait(barrier, count)

    halves = (out_weight.shape[2] // 2, kv_weight.shape[1] // 2)

    def chunk(kind, shard, half):
        size = halves[kind]
        if kind == 0:
            return out_weight.at[shard, :, pl.ds(pl.multiple_of(half * size, 128), size)]
        return kv_weight.at[shard, pl.ds(pl.multiple_of(half * size, 16), size), :]

    def remote(kind, shard, half, sem, target):
        return pltpu.make_async_remote_copy(
            src_ref=chunk(kind, shard, half),
            dst_ref=chunk(kind, shard, half),
            send_sem=sem,
            recv_sem=recv.at[kind, shard, half],
            device_id=target,
            device_id_type=MESH,
        )

    def to_sibling(kind, shard, half):
        return remote(kind, shard, half, sib_send.at[kind, shard // 2, half], sibling)

    def to_x(kind, shard):
        return remote(kind, shard, x, x_send.at[kind, shard // 2], x_peer)

    def to_y(kind, shard, half):
        return remote(kind, shard, half, y_send.at[kind, shard // 4, half], y_peer)

    def to_z(kind, step):
        return remote(
            kind, me, x, z_send.at[kind, step], (group, shard_of(along(step), y, core))
        )

    def arrived(kind, shard, half):
        remote(kind, shard, half, local.at[4], sibling).wait_recv()

    def begin(kind):
        for step in range(1, depth):
            to_z(kind, step).start()
        to_y(kind, me, x).start()
        to_y(kind, me, 1 - x).start()
        for half in range(2):
            to_sibling(kind, me, half).start()

    def from_z(kind, step):
        shard = shard_of(along(depth - step), y, core)
        arrived(kind, shard, x)
        to_y(kind, shard, x).start()
        to_x(kind, shard).start()
        to_sibling(kind, shard, x).start()

    def from_own_y(kind):
        shard = shard_of(z, 1 - y, core)
        arrived(kind, shard, x)
        to_sibling(kind, shard, x).start()
        arrived(kind, shard, 1 - x)
        to_sibling(kind, shard, 1 - x).start()

    def from_y(kind, step):
        shard = shard_of(along(depth - step), 1 - y, core)
        arrived(kind, shard, x)
        to_x(kind, shard).start()
        to_sibling(kind, shard, x).start()

    def from_x(kind, step, row):
        shard = shard_of(along(depth - step), row, core)
        arrived(kind, shard, 1 - x)
        to_sibling(kind, shard, 1 - x).start()

    copies[2].wait()
    to_right = pltpu.make_async_remote_copy(
        src_ref=nearby.at[:, pl.ds(patches, window), :],
        dst_ref=nearby.at[:, pl.ds(0, window), :],
        send_sem=halo_send.at[0],
        recv_sem=halo_recv.at[0],
        device_id=(group, right),
        device_id_type=MESH,
    )
    to_left = pltpu.make_async_remote_copy(
        src_ref=nearby.at[:, pl.ds(window, window), :],
        dst_ref=nearby.at[:, pl.ds(patches + window, window), :],
        send_sem=halo_send.at[1],
        recv_sem=halo_recv.at[1],
        device_id=(group, left),
        device_id_type=MESH,
    )
    to_right.start()
    to_left.start()
    copies[0].wait()
    begin(0)
    copies[1].wait()
    begin(1)

    copies[3].wait()
    block = 32

    def norm_text(i, carry):
        at = pl.ds(pl.multiple_of(i * block, block), block)
        values = text_rows[at, :].astype(jnp.float32)
        square = jnp.mean(values * values, axis=1, keepdims=True)
        rows[at, :] = (values * lax.rsqrt(square + norm_epsilon) * gain_ref[...]).astype(
            jnp.bfloat16
        )
        return carry

    lax.fori_loop(0, text_count // block, norm_text, 0)
    attended[...] = jnp.zeros_like(attended)
    to_right.wait_recv()
    to_left.wait_recv()

    head_size = vis_width // VIS_HEADS
    score_scale = 1.0 / math.sqrt(head_size)
    span = 256

    def one_head(h, carry):
        first = h * head_size
        start = pl.multiple_of(jnp.minimum((first // 128) * 128, vis_width - span), 128)
        column = start + lax.broadcasted_iota(jnp.int32, (1, span), 1)
        mine = (column >= first) & (column < first + head_size)
        query = query_ref[:, pl.ds(start, span)].astype(jnp.float32)
        query = jnp.where(mine, query, 0.0).astype(jnp.bfloat16)
        scores = lax.dot_general(
            query,
            nearby[0, :, pl.ds(start, span)],
            (((1,), (1,)), ((), ())),
            preferred_element_type=jnp.float32,
        )
        scores = jnp.where(
            query_id_ref[...] == key_id_ref[...], scores * score_scale, -1e30
        )
        shifted = jnp.exp(scores - jnp.max(scores, axis=1, keepdims=True))
        weights = (shifted / jnp.sum(shifted, axis=1, keepdims=True)).astype(jnp.bfloat16)
        mixed = jnp.dot(
            weights, nearby[1, :, pl.ds(start, span)], preferred_element_type=jnp.float32
        )
        before = attended[:, pl.ds(start, span)].astype(jnp.float32)
        attended[:, pl.ds(start, span)] = jnp.where(mine, mixed, before).astype(
            jnp.bfloat16
        )
        return carry

    third = VIS_HEADS // 4
    lax.fori_loop(0, third, one_head, 0)
    for step in range(1, depth):
        from_z(0, step)
    lax.fori_loop(third, 2 * third, one_head, 0)
    from_own_y(0)
    for step in range(1, depth):
        from_y(0, step)
        from_x(0, step, y)
    lax.fori_loop(2 * third, 3 * third, one_head, 0)
    for step in range(1, depth):
        from_x(0, step, 1 - y)
    from_z(1, 1)
    lax.fori_loop(3 * third, 4 * third, one_head, 0)
    for level in range(depth):
        for row in range(2):
            for half in range(2):
                arrived(0, shard_of(level, row, 1 - core), half)

    hidden = out_bias_ref[...] + residual_ref[...].astype(jnp.float32)
    head_rows = out_weight.shape[1]
    weight = out_weight[...].reshape(count * head_rows, vis_width)
    hidden = jnp.dot(attended[...], weight, preferred_element_type=jnp.float32) + hidden
    hidden = hidden.astype(jnp.bfloat16)
    for part in range(2):
        outgoing[:, :, pl.ds(part * vis_width, vis_width)] = (
            jnp.dot(place_ref[part], hidden, preferred_element_type=jnp.float32)
            .astype(jnp.bfloat16)
            .reshape(count, 16, vis_width)
        )

    def row_copy(target, source):
        return pltpu.make_async_remote_copy(
            src_ref=outgoing.at[target],
            dst_ref=incoming.at[me],
            send_sem=row_send.at[target],
            recv_sem=row_recv.at[source],
            device_id=(group, target),
            device_id_type=MESH,
        )

    for step in range(1, count):
        row_copy(lax.rem(me + step, count), me).start()
    keep = pltpu.make_async_copy(outgoing.at[me], incoming.at[me], local.at[5])
    keep.start()

    from_own_y(1)
    for step in range(1, depth):
        if step > 1:
            from_z(1, step)
        from_y(1, step)
        from_x(1, step, y)

    keep.wait()
    for step in range(1, count):
        source = lax.rem(me + step, count)
        pltpu.make_async_remote_copy(
            src_ref=outgoing.at[source],
            dst_ref=incoming.at[source],
            send_sem=row_send.at[source],
            recv_sem=row_recv.at[source],
            device_id=(group, source),
            device_id_type=MESH,
        ).wait_recv()
    pair = 4
    for i in range(count // pair):
        values = incoming[pl.ds(i * pair, pair)].astype(jnp.float32)
        low = values[:, :8, :].reshape(pair * 8, width // 2)
        high = values[:, 8:, :].reshape(pair * 8, width // 2)
        square = (
            jnp.sum(low * low, axis=1, keepdims=True)
            + jnp.sum(high * high, axis=1, keepdims=True)
        ) / width
        scale = lax.rsqrt(square + norm_epsilon)
        at = pl.ds(text_count + i * pair * 8, pair * 8)
        gain = gain_ref[...]
        rows[at, : width // 2] = (low * scale * gain[:, : width // 2]).astype(jnp.bfloat16)
        rows[at, width // 2 :] = (high * scale * gain[:, width // 2 :]).astype(jnp.bfloat16)

    pieces = 4
    piece = width // pieces

    def project(number):
        total[...] = jnp.zeros_like(total)

        def add(k, carry):
            at = pl.ds(pl.multiple_of(k * piece, 128), piece)
            weight = jnp.concatenate(
                [kv_weight[2 * number, at, :], kv_weight[2 * number + 1, at, :]], axis=1
            )
            total[...] += jnp.dot(rows[:, at], weight, preferred_element_type=jnp.float32)
            return carry

        lax.fori_loop(0, pieces, add, 0)
        at = pl.ds(pl.multiple_of(number * 2 * LM_HEAD, 2 * LM_HEAD), 2 * LM_HEAD)
        is_key = number * 2 < KV_HEADS
        cosine = jnp.where(is_key, cosine_ref[...], 1.0)
        sine = jnp.where(is_key, sine_ref[...], 0.0)
        for side in range(2):
            lanes = pl.ds(side * LM_HEAD, LM_HEAD)
            here = pl.ds(
                pl.multiple_of(number * 2 * LM_HEAD + side * LM_HEAD, LM_HEAD), LM_HEAD
            )
            values = total[:, lanes] + bias_ref[:, here]
            turned = values * cosine + pltpu.roll(values, LM_HEAD // 2, 1) * sine
            text_cache_ref[:, here] = turned[:text_count].astype(jnp.bfloat16)
            image_cache_ref[:, here] = turned[text_count:].astype(jnp.bfloat16)

    def sib_arrived(number):
        for half in range(2):
            arrived(1, 2 * number + 1 - core, half)

    for row in range(2):
        number = 2 * z + lax.rem(y + row, 2)
        sib_arrived(number)
        project(number)

    def late(step, carry):
        for row in range(2):
            if row == 1:
                shard = shard_of(along(depth - step), 1 - y, core)
                arrived(1, shard, 1 - x)
                to_sibling(1, shard, 1 - x).start()
            number = 2 * along(depth - step) + lax.rem(y + row, 2)
            sib_arrived(number)
            project(number)
        return carry

    lax.fori_loop(1, depth, late, 0)

    to_right.wait_send()
    to_left.wait_send()
    for step in range(1, count):
        row_copy(lax.rem(me + step, count), me).wait_send()
    for kind in range(2):
        for level in range(depth):
            for row in range(2):
                for half in range(2):
                    to_sibling(kind, shard_of(level, row, core), half).wait_send()
        to_y(kind, me, x).wait_send()
        to_y(kind, me, 1 - x).wait_send()
        for step in range(1, depth):
            to_z(kind, step).wait_send()
            near = shard_of(along(step), y, core)
            to_y(kind, near, x).wait_send()
            to_x(kind, near).wait_send()
            to_x(kind, shard_of(along(step), 1 - y, core)).wait_send()


def turns(positions):
    half_size = LM_HEAD // 2
    index_pair = jnp.arange(half_size, dtype=jnp.int32)
    frequency = jnp.power(jnp.float32(rope_base), -2.0 * index_pair.astype(jnp.float32) / LM_HEAD)
    section = (index_pair >= half_size // 4).astype(jnp.int32) + (
        index_pair >= half_size // 4 + 3 * half_size // 8
    ).astype(jnp.int32)
    places = positions.astype(jnp.float32)
    chosen = jnp.where(
        section[None, :] == 0,
        places[0][:, None],
        jnp.where(section[None, :] == 1, places[1][:, None], places[2][:, None]),
    )
    angles = chosen * frequency[None, :]
    cosine, sine_part = jnp.cos(angles), jnp.sin(angles)
    return (
        jnp.concatenate([cosine, cosine], axis=1),
        jnp.concatenate([-sine_part, sine_part], axis=1),
    )


def fused(
    vis_query,
    vis_keyvalue,
    vis_residual,
    vis_out_weight,
    vis_out_bias,
    image_units,
    text_embed,
    lm_gain,
    lm_kv_weight,
    lm_kv_bias,
    text_positions,
    image_destination,
    image_positions,
):
    count = lax.axis_size("tok")
    me = lax.axis_index("tok")
    patches, vis_width = vis_query.shape
    text_count, width = text_embed.shape
    slots = image_positions.shape[1]
    kv_width = lm_kv_bias.shape[0]
    bounds = jnp.concatenate([jnp.zeros((1,), jnp.int32), running_sums(4 * image_units)])
    offset = me * patches
    query_ids = segment_ids(offset + jnp.arange(patches, dtype=jnp.int32), bounds)
    key_ids = segment_ids(
        offset - patches // 2 + jnp.arange(2 * patches, dtype=jnp.int32), bounds
    )
    target = image_destination[:, 0]
    unit = jnp.arange(target.shape[0], dtype=jnp.int32)
    rank = jnp.sum(
        ((target[:, None] == target[None, :]) & (unit[None, :] < unit[:, None])).astype(jnp.int32),
        axis=1,
    )
    patch = jnp.arange(patches, dtype=jnp.int32)
    line = jnp.repeat(target * 16 + rank, 4) + 8 * (lax.rem(patch, 4) // 2)
    lines = jnp.arange(count * 16, dtype=jnp.int32)
    place = jnp.stack(
        [
            (lines[:, None] == line[None, :]) & (lax.rem(patch, 2) == part)[None, :]
            for part in range(2)
        ]
    ).astype(jnp.bfloat16)
    positions = jnp.concatenate(
        [jnp.broadcast_to(text_positions[None, :], (3, text_count)), image_positions], axis=1
    )
    cosine, sine_part = turns(positions)
    depth = count // 4
    vmem = pl.BlockSpec(memory_space=pltpu.VMEM)
    hbm = pl.BlockSpec(memory_space=pl.ANY)
    bf16, f32 = jnp.bfloat16, jnp.float32
    dma = pltpu.SemaphoreType.DMA
    return pl.pallas_call(
        functools.partial(fused_kernel, (count, depth)),
        out_shape=(
            jax.ShapeDtypeStruct((text_count, kv_width), bf16),
            jax.ShapeDtypeStruct((slots, kv_width), bf16),
        ),
        in_specs=[vmem, hbm] + [vmem] * 9 + [hbm] * 3,
        out_specs=(vmem, vmem),
        scratch_shapes=[
            pltpu.VMEM((count,) + vis_out_weight.shape, bf16),
            pltpu.VMEM((count,) + lm_kv_weight.shape, bf16),
            pltpu.VMEM((2, 2 * patches, vis_width), bf16),
            pltpu.VMEM((patches, vis_width), bf16),
            pltpu.VMEM((text_count, width), bf16),
            pltpu.VMEM((text_count + slots, width), bf16),
            pltpu.VMEM((count, 16, width // 2), bf16),
            pltpu.VMEM((count, 16, width // 2), bf16),
            pltpu.VMEM((text_count + slots, 2 * LM_HEAD), f32),
            dma((2, count // 2, 2)),
            dma((2, count // 2)),
            dma((2, count // 4, 2)),
            dma((2, depth)),
            dma((2, count, 2)),
            dma((2,)),
            dma((2,)),
            dma((count,)),
            dma((count,)),
            dma((6,)),
        ],
        compiler_params=pltpu.CompilerParams(
            collective_id=0, has_side_effects=True, vmem_limit_bytes=58 * 2**20
        ),
    )(
        vis_query,
        vis_keyvalue,
        vis_residual,
        vis_out_bias[None, :],
        query_ids[:, None],
        key_ids[None, :],
        place,
        lm_gain[None, :],
        lm_kv_bias[None, :],
        cosine,
        sine_part,
        text_embed,
        vis_out_weight,
        lm_kv_weight,
    )


def choose(*arrays):
    count = lax.axis_size("tok")
    whole_tiles = (
        lax.axis_size("groups") == 2
        and count % 4 == 0
        and arrays[0].shape[0] == 4 * arrays[11].shape[0]
        and arrays[3].shape[0] % 16 == 0
        and arrays[8].shape[1] == LM_HEAD
        and arrays[12].shape[1] == 8 * count
    )
    return fused(*arrays) if whole_tiles else per_device(*arrays)


def solution(mesh):
    placed = (
        P(("groups", "tok"), None),
        P(None, ("groups", "tok"), None),
        P(("groups", "tok"), None),
        P("tok", None),
        P(),
        P("groups"),
        P(("groups", "tok"), None),
        P(),
        P(None, "tok"),
        P(),
        P(("groups", "tok")),
        P(("groups", "tok"), None),
        P(None, ("groups", "tok")),
    )
    return jax.shard_map(
        choose,
        mesh=mesh,
        in_specs=placed,
        out_specs=(P(("groups", "tok"), None), P(("groups", "tok"), None)),
        check_vma=False,
    )
```

```python
import functools
import math

import jax
import jax.numpy as jnp
from jax import lax
from jax.experimental import pallas as pl
from jax.experimental.pallas import tpu as pltpu
from jax.sharding import PartitionSpec as P

VIS_HEADS = 16
KV_HEADS = 8
LM_HEAD = 128


norm_epsilon = 1e-06
rope_base = 1000000.0


def with_halo(block, sides, width):
    for axis, dim in sides:
        count = lax.axis_size(axis)
        forward = [(i, i + 1) for i in range(count - 1)]
        backward = [(target, source) for source, target in forward]
        low = lax.ppermute(
            lax.slice_in_dim(block, block.shape[dim] - width, None, axis=dim), axis, forward
        )
        high = lax.ppermute(lax.slice_in_dim(block, 0, width, axis=dim), axis, backward)
        block = jnp.concatenate([low, block, high], axis=dim)
    return block


def running_sums(counts):
    index = jnp.arange(counts.shape[0], dtype=jnp.int32)
    return jnp.sum(jnp.where(index[None, :] <= index[:, None], counts[None, :], 0), axis=1)


def segment_ids(global_index, bounds):
    return jnp.sum((global_index[:, None] >= bounds[None, :]).astype(jnp.int32), axis=1) - 1


def rms_scale(rows, gain):
    values = rows.astype(jnp.float32)
    mean_square = jnp.mean(values * values, axis=1, keepdims=True)
    return (values * lax.rsqrt(mean_square + norm_epsilon) * gain).astype(jnp.bfloat16)


def rotate_keys(values, bias, positions):
    shifted = values + bias
    row_count = shifted.shape[0]
    kv_half = shifted.shape[1] // 2
    half_size = LM_HEAD // 2
    key_part = shifted[:, :kv_half].reshape(row_count, KV_HEADS, LM_HEAD)
    lower_half = key_part[:, :, :half_size]
    upper_half = key_part[:, :, half_size:]
    index_pair = jnp.arange(half_size, dtype=jnp.int32)
    frequency = jnp.power(jnp.float32(rope_base), -2.0 * index_pair.astype(jnp.float32) / LM_HEAD)
    section = (index_pair >= half_size // 4).astype(jnp.int32) + (
        index_pair >= half_size // 4 + 3 * half_size // 8
    ).astype(jnp.int32)
    places = positions.astype(jnp.float32)
    chosen = jnp.zeros((row_count, half_size), jnp.float32)
    for axis_number in range(3):
        chosen = (
            chosen
            + places[axis_number][:, None] * (section == axis_number).astype(jnp.float32)[None, :]
        )
    angles = chosen * frequency[None, :]
    cosine = jnp.cos(angles)[:, None, :]
    sine_part = jnp.sin(angles)[:, None, :]
    turned = jnp.concatenate(
        [
            lower_half * cosine - upper_half * sine_part,
            upper_half * cosine + lower_half * sine_part,
        ],
        axis=2,
    )
    return jnp.concatenate(
        [turned.reshape(row_count, kv_half), shifted[:, kv_half:]], axis=1
    ).astype(jnp.bfloat16)


def head_attention(query_head, key_head, value_head, allowed, score_scale):
    scores = (
        jnp.einsum("qd,kd->qk", query_head, key_head, preferred_element_type=jnp.float32)
        * score_scale
    )
    scores = jnp.where(allowed, scores, -1e30)
    row_max = jnp.max(scores, axis=1, keepdims=True)
    shifted = jnp.exp(scores - row_max)
    weights = (shifted / jnp.sum(shifted, axis=1, keepdims=True)).astype(jnp.bfloat16)
    return jnp.dot(weights, value_head, preferred_element_type=jnp.float32).astype(jnp.bfloat16)


def project_rows(normed, kv_weight):
    return jnp.dot(
        normed,
        lax.all_gather(kv_weight, "tok", axis=1, tiled=True),
        preferred_element_type=jnp.float32,
    )


def per_device(
    vis_query,
    vis_keyvalue,
    vis_residual,
    vis_out_weight,
    vis_out_bias,
    image_units,
    text_embed,
    lm_gain,
    lm_kv_weight,
    lm_kv_bias,
    text_positions,
    image_destination,
    image_positions,
):
    patch_count, vis_width = vis_query.shape
    head_size = vis_width // VIS_HEADS
    half_window = patch_count // 2
    device_count = lax.axis_size("tok")
    device_index = lax.axis_index("tok")
    nearby = with_halo(vis_keyvalue, (("tok", 1),), half_window)
    bounds = jnp.concatenate([jnp.zeros((1,), jnp.int32), running_sums(4 * image_units)])
    offset = device_index * patch_count
    query_ids = segment_ids(offset + jnp.arange(patch_count, dtype=jnp.int32), bounds)
    key_ids = segment_ids(
        offset - half_window + jnp.arange(2 * patch_count, dtype=jnp.int32), bounds
    )
    allowed = query_ids[:, None] == key_ids[None, :]
    score_scale = 1.0 / math.sqrt(head_size)
    query_heads = vis_query.reshape(patch_count, VIS_HEADS, head_size).transpose(1, 0, 2)
    key_heads = nearby[0].reshape(2 * patch_count, VIS_HEADS, head_size).transpose(1, 0, 2)
    value_heads = nearby[1].reshape(2 * patch_count, VIS_HEADS, head_size).transpose(1, 0, 2)
    attended = lax.map(
        lambda pieces: head_attention(pieces[0], pieces[1], pieces[2], allowed, score_scale),
        (query_heads, key_heads, value_heads),
    )
    attended = attended.transpose(1, 0, 2).reshape(patch_count, vis_width)
    projected = jnp.dot(
        attended,
        lax.all_gather(vis_out_weight, "tok", axis=0, tiled=True),
        preferred_element_type=jnp.float32,
    )
    vis_hidden = (projected + vis_out_bias + vis_residual.astype(jnp.float32)).astype(jnp.bfloat16)
    merged = vis_hidden.reshape(patch_count // 4, 4 * vis_width)
    target = image_destination[:, 0]
    unit_count = target.shape[0]
    same_target = target[:, None] == target[None, :]
    earlier = (
        jnp.arange(unit_count, dtype=jnp.int32)[None, :]
        < jnp.arange(unit_count, dtype=jnp.int32)[:, None]
    )
    slot_rank = jnp.sum((same_target & earlier).astype(jnp.int32), axis=1)
    slot_count = image_positions.shape[1]
    capacity = slot_count // device_count
    slot_index = target * capacity + slot_rank
    text_count = text_embed.shape[0]
    kv_width = lm_kv_bias.shape[0]
    normed = rms_scale(jnp.concatenate([text_embed, merged], axis=0), lm_gain)
    projected_rows = project_rows(normed, lm_kv_weight)
    text_values = projected_rows[:text_count]
    outgoing = (
        jnp.zeros((slot_count, kv_width), jnp.float32)
        .at[slot_index]
        .set(projected_rows[text_count:])
    )
    image_values = lax.all_to_all(outgoing, "tok", split_axis=0, concat_axis=0, tiled=True)
    text_cache = rotate_keys(
        text_values, lm_kv_bias, jnp.broadcast_to(text_positions[None, :], (3, text_count))
    )
    image_cache = rotate_keys(image_values, lm_kv_bias, image_positions)
    return (text_cache, image_cache)


MESH = pl.DeviceIdType.MESH


def fused_kernel(
    dims,
    query_ref,
    keyvalue_ref,
    residual_ref,
    out_bias_ref,
    query_id_ref,
    key_id_ref,
    place_ref,
    gain_ref,
    bias_ref,
    cosine_ref,
    sine_ref,
    text_ref,
    out_shard_ref,
    kv_shard_ref,
    text_cache_ref,
    image_cache_ref,
    out_weight,
    kv_weight,
    nearby,
    attended,
    text_rows,
    rows,
    outgoing,
    incoming,
    total,
    sib_send,
    x_send,
    y_send,
    z_send,
    recv,
    halo_send,
    halo_recv,
    row_send,
    row_recv,
    local,
):
    count, depth, ranges = dims
    kinds = ranges + 1
    group = lax.axis_index("groups")
    me = lax.axis_index("tok")
    core = lax.rem(me, 2)
    chip = me // 2
    y = lax.rem(chip, 2)
    z = chip // 2
    x = group
    sibling = (group, me + 1 - 2 * core)
    x_peer = (1 - group, me)
    y_peer = (group, me + 2 - 4 * y)
    right = lax.rem(me + 1, count)
    left = lax.rem(me + count - 1, count)
    patches, vis_width = query_ref.shape
    window = patches // 2
    text_count, width = text_ref.shape
    slots = image_cache_ref.shape[0]

    def along(step):
        return lax.rem(z + step, depth)

    def shard_of(level, row, lane):
        return (level * 2 + row) * 2 + lane

    copies = [
        pltpu.make_async_copy(out_shard_ref, out_weight.at[me], local.at[0]),
        pltpu.make_async_copy(kv_shard_ref, kv_weight.at[me], local.at[1]),
        pltpu.make_async_copy(
            keyvalue_ref, nearby.at[:, pl.ds(window, patches), :], local.at[2]
        ),
        pltpu.make_async_copy(text_ref, text_rows, local.at[3]),
    ]
    for copy in copies:
        copy.start()

    barrier = pltpu.get_barrier_semaphore()
    for step in range(1, count):
        pl.semaphore_signal(
            barrier,
            inc=1,
            device_id=(group, lax.rem(me + step, count)),
            device_id_type=MESH,
        )
    pl.semaphore_signal(barrier, inc=1, device_id=x_peer, device_id_type=MESH)
    pl.semaphore_wait(barrier, count)

    part_rows = kv_weight.shape[1] // ranges
    halves = (out_weight.shape[2] // 2, part_rows // 2)

    def chunk(kind, shard, half):
        size = halves[min(kind, 1)]
        if kind == 0:
            return out_weight.at[shard, :, pl.ds(pl.multiple_of(half * size, 128), size)]
        first = pl.multiple_of((kind - 1) * part_rows + half * size, 16)
        return kv_weight.at[shard, pl.ds(first, size), :]

    def remote(kind, shard, half, sem, target):
        return pltpu.make_async_remote_copy(
            src_ref=chunk(kind, shard, half),
            dst_ref=chunk(kind, shard, half),
            send_sem=sem,
            recv_sem=recv.at[kind, shard, half],
            device_id=target,
            device_id_type=MESH,
        )

    def to_sibling(kind, shard, half):
        return remote(kind, shard, half, sib_send.at[kind, shard // 2, half], sibling)

    def to_x(kind, shard):
        return remote(kind, shard, x, x_send.at[kind, shard // 2], x_peer)

    def to_y(kind, shard, half):
        return remote(kind, shard, half, y_send.at[kind, shard // 4, half], y_peer)

    def to_z(kind, step):
        return remote(
            kind, me, x, z_send.at[kind, step], (group, shard_of(along(step), y, core))
        )

    def arrived(kind, shard, half):
        remote(kind, shard, half, local.at[4], sibling).wait_recv()

    def begin_z(kind):
        for step in range(1, depth):
            to_z(kind, step).start()

    def begin_y(kind):
        to_y(kind, me, x).start()
        to_y(kind, me, 1 - x).start()
        for half in range(2):
            to_sibling(kind, me, half).start()

    def over_y(kind, step):
        return kind % 2 == 1 and step == 1

    def from_z(kind, step):
        shard = shard_of(along(depth - step), y, core)
        arrived(kind, shard, x)
        to_y(kind, shard, x).start()
        to_x(kind, shard).start()
        to_sibling(kind, shard, x).start()

    def from_own_y(kind):
        shard = shard_of(z, 1 - y, core)
        arrived(kind, shard, x)
        to_sibling(kind, shard, x).start()
        arrived(kind, shard, 1 - x)
        to_sibling(kind, shard, 1 - x).start()

    def from_y(kind, step):
        shard = shard_of(along(depth - step), 1 - y, core)
        arrived(kind, shard, x)
        if not over_y(kind, step):
            to_x(kind, shard).start()
        to_sibling(kind, shard, x).start()

    def from_near_x(kind, step):
        shard = shard_of(along(depth - step), y, core)
        arrived(kind, shard, 1 - x)
        if over_y(kind, step):
            to_y(kind, shard, 1 - x).start()
        to_sibling(kind, shard, 1 - x).start()

    def from_far(kind, step):
        shard = shard_of(along(depth - step), 1 - y, core)
        arrived(kind, shard, 1 - x)
        to_sibling(kind, shard, 1 - x).start()

    def tick(now):
        if now < kinds:
            for step in range(1, depth):
                from_z(now, step)
        if 0 <= now - 1 < kinds:
            from_own_y(now - 1)
            for step in range(1, depth):
                from_y(now - 1, step)
                from_near_x(now - 1, step)
        if 0 <= now - 2 < kinds:
            for step in range(1, depth):
                from_far(now - 2, step)

    copies[2].wait()
    to_right = pltpu.make_async_remote_copy(
        src_ref=nearby.at[:, pl.ds(patches, window), :],
        dst_ref=nearby.at[:, pl.ds(0, window), :],
        send_sem=halo_send.at[0],
        recv_sem=halo_recv.at[0],
        device_id=(group, right),
        device_id_type=MESH,
    )
    to_left = pltpu.make_async_remote_copy(
        src_ref=nearby.at[:, pl.ds(window, window), :],
        dst_ref=nearby.at[:, pl.ds(patches + window, window), :],
        send_sem=halo_send.at[1],
        recv_sem=halo_recv.at[1],
        device_id=(group, left),
        device_id_type=MESH,
    )
    to_right.start()
    to_left.start()
    copies[0].wait()
    begin_z(0)
    begin_y(0)
    copies[1].wait()
    for kind in range(1, kinds):
        begin_z(kind)

    copies[3].wait()
    block = 32

    def norm_text(i, carry):
        at = pl.ds(pl.multiple_of(i * block, block), block)
        values = text_rows[at, :].astype(jnp.float32)
        square = jnp.mean(values * values, axis=1, keepdims=True)
        rows[at, :] = (values * lax.rsqrt(square + norm_epsilon) * gain_ref[...]).astype(
            jnp.bfloat16
        )
        return carry

    lax.fori_loop(0, text_count // block, norm_text, 0)
    attended[...] = jnp.zeros_like(attended)
    to_right.wait_recv()
    to_left.wait_recv()

    head_size = vis_width // VIS_HEADS
    score_scale = 1.0 / math.sqrt(head_size)
    span = 256

    def one_head(h, carry):
        first = h * head_size
        start = pl.multiple_of(jnp.minimum((first // 128) * 128, vis_width - span), 128)
        column = start + lax.broadcasted_iota(jnp.int32, (1, span), 1)
        mine = (column >= first) & (column < first + head_size)
        query = query_ref[:, pl.ds(start, span)].astype(jnp.float32)
        query = jnp.where(mine, query, 0.0).astype(jnp.bfloat16)
        scores = lax.dot_general(
            query,
            nearby[0, :, pl.ds(start, span)],
            (((1,), (1,)), ((), ())),
            preferred_element_type=jnp.float32,
        )
        scores = jnp.where(
            query_id_ref[...] == key_id_ref[...], scores * score_scale, -1e30
        )
        shifted = jnp.exp(scores - jnp.max(scores, axis=1, keepdims=True))
        weights = (shifted / jnp.sum(shifted, axis=1, keepdims=True)).astype(jnp.bfloat16)
        mixed = jnp.dot(
            weights, nearby[1, :, pl.ds(start, span)], preferred_element_type=jnp.float32
        )
        before = attended[:, pl.ds(start, span)].astype(jnp.float32)
        attended[:, pl.ds(start, span)] = jnp.where(mine, mixed, before).astype(
            jnp.bfloat16
        )
        return carry

    fourth = VIS_HEADS // 4
    lax.fori_loop(0, fourth, one_head, 0)
    tick(0)
    for kind in range(1, kinds):
        begin_y(kind)
    lax.fori_loop(fourth, 2 * fourth, one_head, 0)
    tick(1)
    lax.fori_loop(2 * fourth, 3 * fourth, one_head, 0)
    tick(2)
    lax.fori_loop(3 * fourth, 4 * fourth, one_head, 0)
    for level in range(depth):
        for row in range(2):
            for half in range(2):
                arrived(0, shard_of(level, row, 1 - core), half)

    hidden = out_bias_ref[...] + residual_ref[...].astype(jnp.float32)
    head_rows = out_weight.shape[1]
    weight = out_weight[...].reshape(count * head_rows, vis_width)
    hidden = jnp.dot(attended[...], weight, preferred_element_type=jnp.float32) + hidden
    hidden = hidden.astype(jnp.bfloat16)
    for part in range(2):
        outgoing[:, :, pl.ds(part * vis_width, vis_width)] = (
            jnp.dot(place_ref[part], hidden, preferred_element_type=jnp.float32)
            .astype(jnp.bfloat16)
            .reshape(count, 16, vis_width)
        )

    def row_copy(target, source):
        return pltpu.make_async_remote_copy(
            src_ref=outgoing.at[target],
            dst_ref=incoming.at[me],
            send_sem=row_send.at[target],
            recv_sem=row_recv.at[source],
            device_id=(group, target),
            device_id_type=MESH,
        )

    for step in range(1, count):
        row_copy(lax.rem(me + step, count), me).start()
    keep = pltpu.make_async_copy(outgoing.at[me], incoming.at[me], local.at[5])
    keep.start()

    tick(3)
    keep.wait()
    for step in range(1, count):
        source = lax.rem(me + step, count)
        pltpu.make_async_remote_copy(
            src_ref=outgoing.at[source],
            dst_ref=incoming.at[source],
            send_sem=row_send.at[source],
            recv_sem=row_recv.at[source],
            device_id=(group, source),
            device_id_type=MESH,
        ).wait_recv()
    pair = 4
    for i in range(count // pair):
        values = incoming[pl.ds(i * pair, pair)].astype(jnp.float32)
        low = values[:, :8, :].reshape(pair * 8, width // 2)
        high = values[:, 8:, :].reshape(pair * 8, width // 2)
        square = (
            jnp.sum(low * low, axis=1, keepdims=True)
            + jnp.sum(high * high, axis=1, keepdims=True)
        ) / width
        scale = lax.rsqrt(square + norm_epsilon)
        at = pl.ds(text_count + i * pair * 8, pair * 8)
        gain = gain_ref[...]
        rows[at, : width // 2] = (low * scale * gain[:, : width // 2]).astype(jnp.bfloat16)
        rows[at, width // 2 :] = (high * scale * gain[:, width // 2 :]).astype(jnp.bfloat16)

    def multiply(kind):
        depth_at = pl.ds((kind - 1) * part_rows, part_rows)
        for level in range(depth):
            for row in range(2):
                for half in range(2):
                    arrived(kind, shard_of(level, row, 1 - core), half)

        def one_pair(number, carry):
            weight = jnp.concatenate(
                [kv_weight[2 * number, depth_at, :], kv_weight[2 * number + 1, depth_at, :]],
                axis=1,
            )
            product = jnp.dot(rows[:, depth_at], weight, preferred_element_type=jnp.float32)
            if kind > 1:
                product = total[number] + product
            if kind < kinds - 1:
                total[number] = product
                return carry
            is_key = number * 2 < KV_HEADS
            cosine = jnp.where(is_key, cosine_ref[...], 1.0)
            sine = jnp.where(is_key, sine_ref[...], 0.0)
            for side in range(2):
                here = pl.ds(pl.multiple_of((number * 2 + side) * LM_HEAD, LM_HEAD), LM_HEAD)
                values = product[:, side * LM_HEAD : (side + 1) * LM_HEAD] + bias_ref[:, here]
                turned = values * cosine + pltpu.roll(values, LM_HEAD // 2, 1) * sine
                text_cache_ref[:, here] = turned[:text_count].astype(jnp.bfloat16)
                image_cache_ref[:, here] = turned[text_count:].astype(jnp.bfloat16)
            return carry

        lax.fori_loop(0, count // 2, one_pair, 0)

    for now in range(4, kinds + 2):
        tick(now)
        if now - 3 >= 1:
            multiply(now - 3)
    for kind in range(max(1, kinds - 1), kinds):
        multiply(kind)

    to_right.wait_send()
    to_left.wait_send()
    for step in range(1, count):
        row_copy(lax.rem(me + step, count), me).wait_send()
    for kind in range(kinds):
        for level in range(depth):
            for row in range(2):
                for half in range(2):
                    to_sibling(kind, shard_of(level, row, core), half).wait_send()
        to_y(kind, me, x).wait_send()
        to_y(kind, me, 1 - x).wait_send()
        for step in range(1, depth):
            to_z(kind, step).wait_send()
            near = shard_of(along(step), y, core)
            to_y(kind, near, x).wait_send()
            to_x(kind, near).wait_send()
            back = depth - step
            if over_y(kind, step):
                to_y(kind, shard_of(along(back), y, core), 1 - x).wait_send()
            else:
                to_x(kind, shard_of(along(back), 1 - y, core)).wait_send()


def turns(positions):
    half_size = LM_HEAD // 2
    index_pair = jnp.arange(half_size, dtype=jnp.int32)
    frequency = jnp.power(jnp.float32(rope_base), -2.0 * index_pair.astype(jnp.float32) / LM_HEAD)
    section = (index_pair >= half_size // 4).astype(jnp.int32) + (
        index_pair >= half_size // 4 + 3 * half_size // 8
    ).astype(jnp.int32)
    places = positions.astype(jnp.float32)
    chosen = jnp.where(
        section[None, :] == 0,
        places[0][:, None],
        jnp.where(section[None, :] == 1, places[1][:, None], places[2][:, None]),
    )
    angles = chosen * frequency[None, :]
    cosine, sine_part = jnp.cos(angles), jnp.sin(angles)
    return (
        jnp.concatenate([cosine, cosine], axis=1),
        jnp.concatenate([-sine_part, sine_part], axis=1),
    )


def fused(
    vis_query,
    vis_keyvalue,
    vis_residual,
    vis_out_weight,
    vis_out_bias,
    image_units,
    text_embed,
    lm_gain,
    lm_kv_weight,
    lm_kv_bias,
    text_positions,
    image_destination,
    image_positions,
):
    count = lax.axis_size("tok")
    me = lax.axis_index("tok")
    patches, vis_width = vis_query.shape
    text_count, width = text_embed.shape
    slots = image_positions.shape[1]
    kv_width = lm_kv_bias.shape[0]
    bounds = jnp.concatenate([jnp.zeros((1,), jnp.int32), running_sums(4 * image_units)])
    offset = me * patches
    query_ids = segment_ids(offset + jnp.arange(patches, dtype=jnp.int32), bounds)
    key_ids = segment_ids(
        offset - patches // 2 + jnp.arange(2 * patches, dtype=jnp.int32), bounds
    )
    target = image_destination[:, 0]
    unit = jnp.arange(target.shape[0], dtype=jnp.int32)
    rank = jnp.sum(
        ((target[:, None] == target[None, :]) & (unit[None, :] < unit[:, None])).astype(jnp.int32),
        axis=1,
    )
    patch = jnp.arange(patches, dtype=jnp.int32)
    line = jnp.repeat(target * 16 + rank, 4) + 8 * (lax.rem(patch, 4) // 2)
    lines = jnp.arange(count * 16, dtype=jnp.int32)
    place = jnp.stack(
        [
            (lines[:, None] == line[None, :]) & (lax.rem(patch, 2) == part)[None, :]
            for part in range(2)
        ]
    ).astype(jnp.bfloat16)
    positions = jnp.concatenate(
        [jnp.broadcast_to(text_positions[None, :], (3, text_count)), image_positions], axis=1
    )
    cosine, sine_part = turns(positions)
    depth = count // 4
    ranges = 2
    vmem = pl.BlockSpec(memory_space=pltpu.VMEM)
    hbm = pl.BlockSpec(memory_space=pl.ANY)
    bf16, f32 = jnp.bfloat16, jnp.float32
    dma = pltpu.SemaphoreType.DMA
    return pl.pallas_call(
        functools.partial(fused_kernel, (count, depth, ranges)),
        out_shape=(
            jax.ShapeDtypeStruct((text_count, kv_width), bf16),
            jax.ShapeDtypeStruct((slots, kv_width), bf16),
        ),
        in_specs=[vmem, hbm] + [vmem] * 9 + [hbm] * 3,
        out_specs=(vmem, vmem),
        scratch_shapes=[
            pltpu.VMEM((count,) + vis_out_weight.shape, bf16),
            pltpu.VMEM((count,) + lm_kv_weight.shape, bf16),
            pltpu.VMEM((2, 2 * patches, vis_width), bf16),
            pltpu.VMEM((patches, vis_width), bf16),
            pltpu.VMEM((text_count, width), bf16),
            pltpu.VMEM((text_count + slots, width), bf16),
            pltpu.VMEM((count, 16, width // 2), bf16),
            pltpu.VMEM((count, 16, width // 2), bf16),
            pltpu.VMEM((count // 2, text_count + slots, 2 * LM_HEAD), f32),
            dma((ranges + 1, count // 2, 2)),
            dma((ranges + 1, count // 2)),
            dma((ranges + 1, count // 4, 2)),
            dma((ranges + 1, depth)),
            dma((ranges + 1, count, 2)),
            dma((2,)),
            dma((2,)),
            dma((count,)),
            dma((count,)),
            dma((6,)),
        ],
        compiler_params=pltpu.CompilerParams(
            collective_id=0, has_side_effects=True, vmem_limit_bytes=58 * 2**20
        ),
    )(
        vis_query,
        vis_keyvalue,
        vis_residual,
        vis_out_bias[None, :],
        query_ids[:, None],
        key_ids[None, :],
        place,
        lm_gain[None, :],
        lm_kv_bias[None, :],
        cosine,
        sine_part,
        text_embed,
        vis_out_weight,
        lm_kv_weight,
    )


def choose(*arrays):
    count = lax.axis_size("tok")
    whole_tiles = (
        lax.axis_size("groups") == 2
        and count % 4 == 0
        and arrays[0].shape[0] == 4 * arrays[11].shape[0]
        and arrays[3].shape[0] % 16 == 0
        and arrays[8].shape[1] == LM_HEAD
        and arrays[12].shape[1] == 8 * count
    )
    return fused(*arrays) if whole_tiles else per_device(*arrays)


def solution(mesh):
    placed = (
        P(("groups", "tok"), None),
        P(None, ("groups", "tok"), None),
        P(("groups", "tok"), None),
        P("tok", None),
        P(),
        P("groups"),
        P(("groups", "tok"), None),
        P(),
        P(None, "tok"),
        P(),
        P(("groups", "tok")),
        P(("groups", "tok"), None),
        P(None, ("groups", "tok")),
    )
    return jax.shard_map(
        choose,
        mesh=mesh,
        in_specs=placed,
        out_specs=(P(("groups", "tok"), None), P(("groups", "tok"), None)),
        check_vma=False,
    )
```
